32 devices in a mesh: groups: 2 (over y), pairs: 4 (over z), rhs: 4 (over x, core).
Axes of the slice: x: 2, y: 2, z: 4, core: 2. Of those that a mesh axis runs over, the one named last changes fastest.
Arguments:
- features: float32 [40, 12288], P(None, ('groups', 'pairs')), parts along dimension 1
- inv_scale: float32 [40], replicated, may hold values from 0.006 to 0.018
- cluster_order: int32 [12288], P(('groups', 'pairs')), parts along dimension 0, may hold values from 0 to 6143, as said below
- counts: int32 [8], P(('groups', 'pairs')), parts along dimension 0, may hold values from 384 to 1536, as said below
- tile_cols: int32 [24, 3], P('groups'), parts along dimension 0, may hold values from -1 to 11, as said below
- targets: float32 [32, 12288], P('rhs', ('groups', 'pairs')), parts along dimension 1, may hold values from -4 to 4
Outputs:
- solution: float32 [32, 12288], P('rhs', ('groups', 'pairs')), parts along dimension 1
- residual: float32 [32, 12288], P('rhs', ('groups', 'pairs')), parts along dimension 1
The draws below stay inside these ranges and needn't reach their ends.
There are 2 independent parts, one for each index of `groups`. The reference program is written for one: setup_inputs(seed, part) draws one part's arguments, and reference() takes and returns one part's arrays. A program takes and returns all parts, laid end to end along the dimension named above; an argument that names none is the same for every part. Nothing has to cross between parts.
Inputs may be any that keep to these rules, and one draw needn't show every extreme that they name: `cluster_order`: each block of 1536 positions of the cluster ordering holds a permutation of the same block of input columns. `counts`: some block is full in every draw. `tile_cols`: row tile i lists i first, then 3 - 1 distinct tiles from i + 1 to i + 3; a tile past the last one is given as -1.
All inputs are finite; a program needn't handle non-finite values.
Results may differ from the reference program's by a relative error of at most 0.0003.
Values sent between devices are 32-bit elements; how exact they have to be, the bound alone decides.
A program may use at most 64 MiB of HBM per device.

```python
import math
import jax
import jax.numpy as jnp
from jax import lax

F = 40
R = 32
TILE = 512
BAND = 3
ITERS = 2
P_DEV = 1536
SHARDS = 4
TILES = 12
TOTAL = 6144


noise_gain = 4.0


def order_helper(key):
    subkeys = jax.random.split(jax.random.fold_in(key, 7), SHARDS)
    blocks = jax.vmap(lambda subkey: jax.random.permutation(subkey, P_DEV))(subkeys)
    offsets = jnp.arange(SHARDS, dtype=jnp.int32)[:, None] * P_DEV
    return (blocks.astype(jnp.int32) + offsets).reshape(-1).astype(jnp.int32)


def draw_cluster_order(key, part):
    return order_helper(key)


def draw_features(key, part):
    order = order_helper(key)
    inverse = jnp.zeros((TOTAL,), jnp.int32).at[order].set(jnp.arange(TOTAL, dtype=jnp.int32))
    first, second, third, fourth = jax.random.split(jax.random.fold_in(key, 11), 4)
    place = inverse.astype(jnp.float32)[None, :]
    phase = jax.random.uniform(first, (F, 1), jnp.float32, -math.pi, math.pi)
    height = jax.random.uniform(second, (F, 1), jnp.float32, 1.0, 2.0)
    row_gain = jax.random.uniform(third, (1, TOTAL), jnp.float32, 0.5, 1.5)
    noise = jax.random.normal(fourth, (F, TOTAL), jnp.float32)
    drift = height * jnp.sin(2.0 * math.pi * place / (16.0 * TILE) + phase)
    return (drift + noise_gain * row_gain * noise).astype(jnp.float32)


def draw_counts(key, part):
    first, second = jax.random.split(jax.random.fold_in(key, 3))
    drawn = jax.random.randint(first, (SHARDS,), P_DEV // 4, P_DEV + 1)
    fullest = jax.random.randint(second, (), 0, SHARDS)
    return jnp.where(jnp.arange(SHARDS) == fullest, P_DEV, drawn).astype(jnp.int32)


def draw_tile_cols(key, part):
    subkeys = jax.random.split(jax.random.fold_in(key, 5), TILES)
    offsets = jax.vmap(lambda subkey: jax.random.permutation(subkey, BAND)[:BAND - 1] + 1)(subkeys)
    rows = jnp.arange(TILES, dtype=jnp.int32)[:, None]
    columns = rows + offsets.astype(jnp.int32)
    columns = jnp.where(columns < TILES, columns, -1)
    return jnp.concatenate([rows, columns], axis=1).astype(jnp.int32)


def draw_targets(key, part):
    first, second = jax.random.split(jax.random.fold_in(key, 13))
    levels = jnp.clip(jax.random.normal(first, (R, TILES, 1), jnp.float32), -3.0, 3.0)
    noise = jnp.clip(0.3 * jax.random.normal(second, (R, TILES, TILE), jnp.float32), -1.0, 1.0)
    return (levels + noise).reshape(R, TOTAL).astype(jnp.float32)


def setup_inputs(seed: int = 0, part: int = 0) -> dict:
    key_list = jax.random.split(jax.random.key(seed), 7)
    own_keys = jax.random.split(jax.random.fold_in(key_list[6], part), 7)
    return {
        "features": draw_features(jax.random.fold_in(jax.random.fold_in(key_list[6], part), 71), part),
        "inv_scale": jnp.clip(jnp.exp(jax.random.uniform(key_list[1], (F,), jnp.float32, math.log(0.006), math.log(0.018))), 0.006, 0.018),
        "cluster_order": draw_cluster_order(jax.random.fold_in(jax.random.fold_in(key_list[6], part), 71), part),
        "counts": draw_counts(jax.random.fold_in(jax.random.fold_in(key_list[6], part), 71), part),
        "tile_cols": draw_tile_cols(jax.random.fold_in(jax.random.fold_in(key_list[6], part), 71), part),
        "targets": draw_targets(jax.random.fold_in(jax.random.fold_in(key_list[6], part), 71), part),
    }


root_three = math.sqrt(3.0)
highest = lax.Precision.HIGHEST

def form_tile(rows_feat, cols_feat):
    inner = lax.dot_general(rows_feat, cols_feat, (((0,), (0,)), ((), ())), precision=highest, preferred_element_type=jnp.float32)
    row_sq = lax.optimization_barrier(jnp.sum(rows_feat * rows_feat, axis=0))
    col_sq = lax.optimization_barrier(jnp.sum(cols_feat * cols_feat, axis=0))
    dist_sq = jnp.maximum(row_sq[:, None] + col_sq[None, :] - 2.0 * inner, 0.0)
    distance = jnp.sqrt(dist_sq + 1e-06)
    envelope = jnp.maximum(1.0 - distance, 0.0)
    return (1.0 + root_three * distance) * jnp.exp(-root_three * distance) * envelope * envelope

def toward_rows(vector, kernel):
    return lax.dot_general(vector, kernel, (((1,), (1,)), ((), ())), precision=highest, preferred_element_type=jnp.float32)

def toward_cols(vector, kernel):
    return jnp.dot(vector, kernel, precision=highest, preferred_element_type=jnp.float32)

def add_block(accum, piece, start):
    current = lax.dynamic_slice_in_dim(accum, start, TILE, 1)
    return lax.dynamic_update_slice_in_dim(accum, current + piece, start, 1)

def reference(features, inv_scale, cluster_order, counts, tile_cols, targets):
    ordered = jnp.take(features, cluster_order, axis=1) * inv_scale[:, None]
    positions = jnp.arange(TOTAL, dtype=jnp.int32)
    live = (positions % P_DEV < jnp.take(counts, positions // P_DEV)).astype(jnp.float32)
    strength = 0.95 / (2 * BAND * TILE)

    def operate(vector):

        def visit_tile(tile_index, accum):
            tile_index = jnp.asarray(tile_index).astype(jnp.int32)
            row_start = (tile_index * TILE).astype(jnp.int32)
            rows_feat = lax.dynamic_slice_in_dim(ordered, row_start, TILE, 1)
            rows_vec = lax.dynamic_slice_in_dim(vector, row_start, TILE, 1)
            for band_slot in range(BAND):
                column = tile_cols[tile_index, band_slot].astype(jnp.int32)
                listed = column >= 0
                col_start = (jnp.maximum(column, 0) * TILE).astype(jnp.int32)
                kernel = form_tile(rows_feat, lax.dynamic_slice_in_dim(ordered, col_start, TILE, 1))
                row_terms = toward_rows(lax.dynamic_slice_in_dim(vector, col_start, TILE, 1), kernel)
                col_terms = toward_cols(rows_vec, kernel)
                accum = add_block(accum, jnp.where(listed, row_terms, 0.0), row_start)
                accum = add_block(accum, jnp.where(listed & (column != tile_index), col_terms, 0.0), col_start)
            return accum
        accum = lax.fori_loop(0, TILES, visit_tile, jnp.zeros(vector.shape, jnp.float32))
        return vector + strength * live[None, :] * accum
    solution = jnp.zeros(targets.shape, jnp.float32)
    residual = targets * live[None, :]
    direction = residual
    norm_now = lax.optimization_barrier(jnp.sum(residual * residual, axis=1))
    for sweep in range(ITERS):
        applied = operate(direction)
        step_size = norm_now / lax.optimization_barrier(jnp.sum(direction * applied, axis=1))
        solution = solution + step_size[:, None] * direction
        residual = residual - step_size[:, None] * applied
        norm_next = lax.optimization_barrier(jnp.sum(residual * residual, axis=1))
        direction = residual + (norm_next / norm_now)[:, None] * direction
        norm_now = norm_next
    return (solution, residual)
```

```python
import functools
import math

import jax
import jax.numpy as jnp
from jax import lax
from jax.experimental import pallas as pl
from jax.experimental.pallas import tpu as pltpu
from jax.sharding import PartitionSpec as P

TILE = 512
BAND = 3
NT = 3
CHUNK = 64
FEAT = 40
DEPTH = 256

root_three = math.sqrt(3.0)
log2_e = math.log2(math.e)
f32 = jnp.float32
bf16 = jnp.bfloat16

OFF = ((0, 1, 0), (0, 2, 1), (1, 2, 0), (1, 3, 1), (2, 3, 0), (2, 4, 1))


def three_parts(x):
    hi = x.astype(bf16).astype(f32)
    rest = x - hi
    mid = rest.astype(bf16).astype(f32)
    low = (rest - mid).astype(bf16).astype(f32)
    return hi, mid, low


def operand(x, is_row):
    hi, mid, low = three_parts(x)
    sq = jnp.sum(x * x, axis=0, keepdims=True)
    sq_hi, sq_mid, sq_low = three_parts(sq)
    width = x.shape[1]
    row = lax.broadcasted_iota(jnp.int32, (8, width), 0)
    first = 0 if is_row else 3
    tail = jnp.where(row < 6, 1.0, 0.0)
    tail = jnp.where(row == first, sq_hi, tail)
    tail = jnp.where(row == first + 1, sq_mid, tail)
    tail = jnp.where(row == first + 2, sq_low, tail)
    zero = jnp.zeros((8, width), f32)
    if is_row:
        parts = [-2.0 * y for y in (hi, hi, mid, hi, low, mid)]
    else:
        parts = [hi, mid, hi, low, hi, mid]
    return jnp.concatenate(parts + [tail, zero], axis=0)


def two_parts(v):
    hi = v.astype(bf16).astype(f32)
    return jnp.concatenate([hi, v - hi], axis=0).astype(bf16)


def fold(t):
    half = t.shape[0] // 2
    return t[:half] + t[half:]


def body(
    n, strength, feat_ref, counts_ref, cols_ref, targ_ref, sol_ref, res_ref,
    up_feat, r_buf, up_r, w_buf, up_w, out1, in1, out2, in2, part1, got1, part2, got2,
    a_ref, b_ref, ds_ref, khi, klo, vec, send_sem, recv_sem, psend1, precv1, psend2, precv2,
):
    me = lax.axis_index("pairs")
    mesh_ids = pl.DeviceIdType.MESH
    p_slots = NT * TILE
    has_up = me < n - 1
    has_down = me > 0

    barrier = pltpu.get_barrier_semaphore()
    for k in range(1, n):
        pl.semaphore_signal(barrier, inc=1, device_id={"pairs": lax.rem(me + k, n)}, device_id_type=mesh_ids)

    lane = lax.broadcasted_iota(jnp.int32, (8, p_slots), 1)
    live = jnp.where(lane < counts_ref[0], 1.0, 0.0)
    r0 = targ_ref[...] * live
    r_buf[...] = r0

    @pl.when(jnp.logical_not(has_up))
    def _():
        up_feat[...] = jnp.zeros_like(up_feat)
        up_r[...] = jnp.zeros_like(up_r)
        up_w[...] = jnp.zeros_like(up_w)

    @pl.when(jnp.logical_not(has_down))
    def _():
        in1[...] = jnp.zeros_like(in1)
        in2[...] = jnp.zeros_like(in2)

    pl.semaphore_wait(barrier, n - 1)

    def shift(src, dst, slot, by):
        return pltpu.make_async_remote_copy(
            src_ref=src, dst_ref=dst, send_sem=send_sem.at[slot], recv_sem=recv_sem.at[slot],
            device_id={"pairs": lax.rem(me + by + n, n)}, device_id_type=mesh_ids,
        )

    c_feat = shift(feat_ref, up_feat, 0, -1)
    c_r = shift(r_buf, up_r, 1, -1)
    c_w = shift(w_buf, up_w, 2, -1)
    c_1 = shift(out1, in1, 3, 1)
    c_2 = shift(out2, in2, 4, 1)

    def when_start(cond, *copies):
        @pl.when(cond)
        def _():
            for c in copies:
                c.start()

    def when_recv(cond, *copies):
        @pl.when(cond)
        def _():
            for c in copies:
                c.wait_recv()

    when_start(has_down, c_r, c_feat)

    base = me * NT
    start, keep0, keep1 = [], [], []
    for row, cand, slot in OFF:
        a = cols_ref[base + row, 1]
        b = cols_ref[base + row, 2]
        a_in = jnp.where(a < 0, row + 3, a - base)
        b_in = jnp.where(b < 0, row + 3, b - base)
        if slot == 0:
            valid = jnp.maximum(a, b) >= 0
            c = jnp.minimum(jnp.minimum(a_in, b_in), cand + 1)
        else:
            valid = jnp.minimum(a, b) >= 0
            c = jnp.maximum(a_in, b_in)
        start.append(c)
        keep0.append(jnp.where(valid & (c == cand), 1.0, 0.0).astype(f32))
        keep1.append(jnp.where(valid & (c == cand + 1), 1.0, 0.0).astype(f32))

    def pick(ref, k, own):
        cand = OFF[k][1]
        lo = ref[:, cand * TILE : (cand + 1) * TILE]
        hi = ref[:, (cand + 1) * TILE : (cand + 2) * TILE]
        return jnp.where(start[k] == cand, lo, hi)

    for i in range(NT):
        span = slice(i * TILE, (i + 1) * TILE)
        x = feat_ref[:, span]
        a_ref[span, :] = operand(x, True).T.astype(bf16)
        b_ref[:, span] = operand(x, False).astype(bf16)

    def form(t, row, cols):
        ds_ref[...] = jnp.dot(a_ref[row * TILE : (row + 1) * TILE, :], cols, preferred_element_type=f32)

        def step(s, carry):
            at = pl.ds(pl.multiple_of(s * CHUNK, CHUNK), CHUNK)
            d2 = jnp.maximum(ds_ref[at, :], 0.0) + 1e-6
            d = d2 * lax.rsqrt(d2)
            env = jnp.maximum(1.0 - d, 0.0)
            k = (1.0 + root_three * d) * jnp.exp2((-root_three * log2_e) * d) * (env * env)
            hi = k.astype(bf16)
            khi[t, at, :] = hi
            klo[t, at, :] = (k - hi.astype(f32)).astype(bf16)
            return carry

        lax.fori_loop(0, TILE // CHUNK, step, 0)

    nt_dims = (((1,), (1,)), ((), ()))

    def to_rows(t, v):
        return fold(
            lax.dot_general(v, khi[t], nt_dims, preferred_element_type=f32)
            + lax.dot_general(v, klo[t], nt_dims, preferred_element_type=f32)
        )

    def to_cols(t, v):
        return fold(
            jnp.dot(v, khi[t], preferred_element_type=f32)
            + jnp.dot(v, klo[t], preferred_element_type=f32)
        )

    for i in range(NT):
        form(i, i, b_ref[:, i * TILE : (i + 1) * TILE])
    form(NT, 0, pick(b_ref, 0, True))
    when_recv(has_up, c_feat)
    for i in range(NT):
        span = slice(i * TILE, (i + 1) * TILE)
        b_ref[:, p_slots + i * TILE : p_slots + (i + 1) * TILE] = operand(up_feat[:, span], False).astype(bf16)
    for k in range(1, 6):
        form(NT + k, OFF[k][0], pick(b_ref, k, False))

    def own(i):
        return vec[:, i * TILE : (i + 1) * TILE]

    def operate(v, out_ref, c_out, up_ref, c_up, in_ref):
        vec[:, :p_slots] = two_parts(v)
        acc = [jnp.zeros((8, TILE), f32) for _ in range(2 * NT)]
        for k in range(1, 6):
            row, cand, _ = OFF[k]
            t = to_cols(NT + k, own(row))
            acc[cand] = acc[cand] + keep0[k] * t
            acc[cand + 1] = acc[cand + 1] + keep1[k] * t
        out_ref[...] = jnp.concatenate(acc[NT:], axis=1)
        when_start(has_up, c_out)
        for i in range(NT):
            acc[i] = acc[i] + to_rows(i, own(i))
        t = to_cols(NT, own(0))
        acc[1] = acc[1] + keep0[0] * t
        acc[2] = acc[2] + keep1[0] * t
        acc[0] = acc[0] + (keep0[0] + keep1[0]) * to_rows(NT, pick(vec, 0, True))
        when_recv(has_up, c_up)
        vec[:, p_slots:] = two_parts(up_ref[...])
        for k in range(1, 6):
            row = OFF[k][0]
            acc[row] = acc[row] + (keep0[k] + keep1[k]) * to_rows(NT + k, pick(vec, k, False))
        when_recv(has_down, c_out)
        total = jnp.concatenate(acc[:NT], axis=1) + in_ref[...]
        return v + strength * live * total

    def start_sums(first, second, part, got, ssem, rsem):
        part[0:8, :] = jnp.broadcast_to(jnp.sum(first, axis=1, keepdims=True), (8, 128))
        part[8:16, :] = jnp.broadcast_to(jnp.sum(second, axis=1, keepdims=True), (8, 128))
        copies = []
        for k in range(1, n):
            c = pltpu.make_async_remote_copy(
                src_ref=part, dst_ref=got.at[k - 1], send_sem=ssem.at[k - 1], recv_sem=rsem.at[k - 1],
                device_id={"pairs": lax.rem(me + k, n)}, device_id_type=mesh_ids,
            )
            c.start()
            copies.append(c)
        return copies

    def end_sums(copies, part, got):
        total = part[...]
        for k, c in enumerate(copies):
            c.wait_recv()
            total = total + got[k]
        return total[0:8, 0:1], total[8:16, 0:1]

    w = operate(r0, out1, c_1, up_r, c_r, in1)
    w_buf[...] = w
    when_start(has_down, c_w)
    sums1 = start_sums(r0 * r0, r0 * w, part1, got1, psend1, precv1)
    u = operate(w, out2, c_2, up_w, c_w, in2)
    norm0, curve0 = end_sums(sums1, part1, got1)
    step0 = norm0 / curve0
    r1 = r0 - step0 * w
    applied = w - step0 * u
    sums2 = start_sums(r1 * r1, r1 * applied, part2, got2, psend2, precv2)
    norm1, curve1 = end_sums(sums2, part2, got2)
    rescale = norm1 / norm0
    step1 = norm1 / (curve1 - rescale * norm1 / step0)
    sol_ref[...] = step0 * r0 + step1 * (r1 + rescale * r0)
    res_ref[...] = r1 - step1 * (applied + rescale * w)

    @pl.when(has_down)
    def _():
        for c in (c_feat, c_r, c_w):
            c.wait_send()

    @pl.when(has_up)
    def _():
        for c in (c_1, c_2):
            c.wait_send()

    for c in sums1 + sums2:
        c.wait_send()


def on_device(n, features, inv_scale, cluster_order, counts, tile_cols, targets):
    p_slots = features.shape[1]
    rhs_rows = targets.shape[0]
    shard_index = lax.axis_index("pairs")
    local_index = cluster_order - shard_index * p_slots
    ordered = jnp.take(features, local_index, axis=1) * inv_scale[:, None]
    strength = 0.95 / (2 * BAND * TILE)
    padded = targets
    if rhs_rows < 8:
        padded = jnp.concatenate([targets, jnp.ones((8 - rhs_rows, p_slots), f32)], axis=0)
    vmem = pl.BlockSpec(memory_space=pltpu.VMEM)
    smem = pl.BlockSpec(memory_space=pltpu.SMEM)
    field = pltpu.VMEM((8, p_slots), f32)
    dma = pltpu.SemaphoreType.DMA
    tiles = 9
    out = jax.ShapeDtypeStruct((8, p_slots), f32)
    sol, res = pl.pallas_call(
        functools.partial(body, n, strength),
        out_shape=(out, out),
        in_specs=[vmem, smem, smem, vmem],
        out_specs=(vmem, vmem),
        scratch_shapes=[
            pltpu.VMEM((FEAT, p_slots), f32),
            field, field, field, field, field, field, field, field,
            pltpu.VMEM((16, 128), f32),
            pltpu.VMEM((n - 1, 16, 128), f32),
            pltpu.VMEM((16, 128), f32),
            pltpu.VMEM((n - 1, 16, 128), f32),
            pltpu.VMEM((p_slots, DEPTH), bf16),
            pltpu.VMEM((DEPTH, 2 * p_slots), bf16),
            pltpu.VMEM((TILE, TILE), f32),
            pltpu.VMEM((tiles, TILE, TILE), bf16),
            pltpu.VMEM((tiles, TILE, TILE), bf16),
            pltpu.VMEM((16, 2 * p_slots), bf16),
            dma((5,)), dma((5,)),
            dma((n - 1,)), dma((n - 1,)), dma((n - 1,)), dma((n - 1,)),
        ],
        compiler_params=pltpu.CompilerParams(
            collective_id=0, has_side_effects=True, vmem_limit_bytes=48 * 2**20
        ),
    )(ordered, counts, tile_cols, padded)
    return sol[:rhs_rows], res[:rhs_rows]


def solution(mesh):
    return jax.shard_map(
        functools.partial(on_device, mesh.shape["pairs"]),
        mesh=mesh,
        in_specs=(
            P(None, ("groups", "pairs")),
            P(),
            P(("groups", "pairs")),
            P(("groups", "pairs")),
            P("groups", None),
            P("rhs", ("groups", "pairs")),
        ),
        out_specs=(P("rhs", ("groups", "pairs")), P("rhs", ("groups", "pairs"))),
        check_vma=False,
    )
```

```python
import functools
import math

import jax
import jax.numpy as jnp
from jax import lax
from jax.experimental import pallas as pl
from jax.experimental.pallas import tpu as pltpu
from jax.sharding import PartitionSpec as P

TILE = 512
BAND = 3
NT = 3
CHUNK = 64
LANES = 128
FEAT = 40
DEPTH = 256

root_three = math.sqrt(3.0)
log2_e = math.log2(math.e)
f32 = jnp.float32
bf16 = jnp.bfloat16

OFF = ((0, 1, 0), (0, 2, 1), (1, 2, 0), (1, 3, 1), (2, 3, 0), (2, 4, 1))


def three_parts(x):
    hi = x.astype(bf16).astype(f32)
    rest = x - hi
    mid = rest.astype(bf16).astype(f32)
    low = (rest - mid).astype(bf16).astype(f32)
    return hi, mid, low


def operand(x, is_row):
    hi, mid, low = three_parts(x)
    sq = jnp.sum(x * x, axis=0, keepdims=True)
    sq_hi, sq_mid, sq_low = three_parts(sq)
    width = x.shape[1]
    row = lax.broadcasted_iota(jnp.int32, (8, width), 0)
    first = 0 if is_row else 3
    tail = jnp.where(row < 6, 1.0, 0.0)
    tail = jnp.where(row == first, sq_hi, tail)
    tail = jnp.where(row == first + 1, sq_mid, tail)
    tail = jnp.where(row == first + 2, sq_low, tail)
    zero = jnp.zeros((8, width), f32)
    if is_row:
        parts = [-2.0 * y for y in (hi, hi, mid, hi, low, mid)]
    else:
        parts = [hi, mid, hi, low, hi, mid]
    return jnp.concatenate(parts + [tail, zero], axis=0)


def two_parts(v):
    hi = v.astype(bf16).astype(f32)
    return jnp.concatenate([hi, v - hi], axis=0).astype(bf16)


def fold(t):
    half = t.shape[0] // 2
    return t[:half] + t[half:]


def body(
    n, strength, raw_ref, scale_ref, order_ref, counts_ref, cols_ref, targ_ref, sol_ref, res_ref,
    feat, up_feat, r_buf, up_r, w_buf, up_w, out1, in1, out2, in2, part1, got1, part2, got2,
    a_ref, b_ref, ds_ref, khi, klo, vec, send_sem, recv_sem, psend1, precv1, psend2, precv2,
):
    me = lax.axis_index("pairs")
    mesh_ids = pl.DeviceIdType.MESH
    p_slots = NT * TILE
    has_up = me < n - 1
    has_down = me > 0

    barrier = pltpu.get_barrier_semaphore()
    for k in range(1, n):
        pl.semaphore_signal(barrier, inc=1, device_id={"pairs": lax.rem(me + k, n)}, device_id_type=mesh_ids)

    lane = lax.broadcasted_iota(jnp.int32, (8, p_slots), 1)
    live = jnp.where(lane < counts_ref[0], 1.0, 0.0)
    r0 = targ_ref[...] * live
    r_buf[...] = r0

    @pl.when(jnp.logical_not(has_up))
    def _():
        up_feat[...] = jnp.zeros_like(up_feat)
        up_r[...] = jnp.zeros_like(up_r)
        up_w[...] = jnp.zeros_like(up_w)

    @pl.when(jnp.logical_not(has_down))
    def _():
        in1[...] = jnp.zeros_like(in1)
        in2[...] = jnp.zeros_like(in2)

    diag = lax.broadcasted_iota(jnp.int32, (FEAT, FEAT), 0) == lax.broadcasted_iota(jnp.int32, (FEAT, FEAT), 1)
    scale = jnp.sum(jnp.where(diag, jnp.broadcast_to(scale_ref[...], (FEAT, FEAT)), 0.0), axis=1, keepdims=True)

    def gather_tile(i):
        for c in range(TILE // LANES):
            first = i * TILE + c * LANES
            index = order_ref[:, first : first + LANES] - me * p_slots
            index = jnp.broadcast_to(index, (FEAT, LANES))
            group = lax.shift_right_logical(index, 7)
            within = jnp.bitwise_and(index, LANES - 1)
            got = jnp.zeros((FEAT, LANES), f32)
            for s in range(p_slots // LANES):
                part = jnp.take_along_axis(raw_ref[:, s * LANES : (s + 1) * LANES], within, axis=1)
                got = jnp.where(group == s, part, got)
            feat[i, :, c * LANES : (c + 1) * LANES] = got * scale

    gather_tile(0)
    pl.semaphore_wait(barrier, n - 1)

    def shift(src, dst, slot, by):
        return pltpu.make_async_remote_copy(
            src_ref=src, dst_ref=dst, send_sem=send_sem.at[slot], recv_sem=recv_sem.at[slot],
            device_id={"pairs": lax.rem(me + by + n, n)}, device_id_type=mesh_ids,
        )

    c_feat = [shift(feat.at[i], up_feat.at[i], 4 + i, -1) for i in range(NT)]
    c_r = shift(r_buf, up_r, 0, -1)
    c_w = shift(w_buf, up_w, 1, -1)
    c_1 = shift(out1, in1, 2, 1)
    c_2 = shift(out2, in2, 3, 1)

    def when_start(cond, *copies):
        @pl.when(cond)
        def _():
            for c in copies:
                c.start()

    def when_recv(cond, *copies):
        @pl.when(cond)
        def _():
            for c in copies:
                c.wait_recv()

    when_start(has_down, c_feat[0])
    gather_tile(1)
    when_start(has_down, c_feat[1])
    gather_tile(2)
    when_start(has_down, c_feat[2], c_r)

    base = me * NT
    start, keep0, keep1 = [], [], []
    for row, cand, slot in OFF:
        a = cols_ref[base + row, 1]
        b = cols_ref[base + row, 2]
        a_in = jnp.where(a < 0, row + 3, a - base)
        b_in = jnp.where(b < 0, row + 3, b - base)
        if slot == 0:
            valid = jnp.maximum(a, b) >= 0
            c = jnp.minimum(jnp.minimum(a_in, b_in), cand + 1)
        else:
            valid = jnp.minimum(a, b) >= 0
            c = jnp.maximum(a_in, b_in)
        start.append(c)
        keep0.append(jnp.where(valid & (c == cand), 1.0, 0.0).astype(f32))
        keep1.append(jnp.where(valid & (c == cand + 1), 1.0, 0.0).astype(f32))

    def pick(ref, k, own):
        cand = OFF[k][1]
        lo = ref[:, cand * TILE : (cand + 1) * TILE]
        hi = ref[:, (cand + 1) * TILE : (cand + 2) * TILE]
        return jnp.where(start[k] == cand, lo, hi)

    for i in range(NT):
        span = slice(i * TILE, (i + 1) * TILE)
        x = feat[i]
        a_ref[span, :] = operand(x, True).T.astype(bf16)
        b_ref[:, span] = operand(x, False).astype(bf16)

    def form(t, row, cols):
        ds_ref[t % 2] = jnp.dot(a_ref[row * TILE : (row + 1) * TILE, :], cols, preferred_element_type=f32)
        for s in range(TILE // CHUNK):
            at = slice(s * CHUNK, (s + 1) * CHUNK)
            d2 = jnp.maximum(ds_ref[t % 2, at, :], 0.0) + 1e-6
            d = d2 * lax.rsqrt(d2)
            env = jnp.maximum(1.0 - d, 0.0)
            k = (1.0 + root_three * d) * jnp.exp2((-root_three * log2_e) * d) * (env * env)
            hi = k.astype(bf16)
            khi[t, at, :] = hi
            klo[t, at, :] = (k - hi.astype(f32)).astype(bf16)

    nt_dims = (((1,), (1,)), ((), ()))

    def to_rows(t, v):
        return fold(
            lax.dot_general(v, khi[t], nt_dims, preferred_element_type=f32)
            + lax.dot_general(v, klo[t], nt_dims, preferred_element_type=f32)
        )

    def to_cols(t, v):
        return fold(
            jnp.dot(v, khi[t], preferred_element_type=f32)
            + jnp.dot(v, klo[t], preferred_element_type=f32)
        )

    for i in range(NT):
        form(i, i, b_ref[:, i * TILE : (i + 1) * TILE])
    form(NT, 0, pick(b_ref, 0, True))
    for i, pairs in ((0, (1, 2)), (1, (3, 4)), (2, (5,))):
        when_recv(has_up, c_feat[i])
        b_ref[:, p_slots + i * TILE : p_slots + (i + 1) * TILE] = operand(up_feat[i], False).astype(bf16)
        for k in pairs:
            form(NT + k, OFF[k][0], pick(b_ref, k, False))

    def own(i):
        return vec[:, i * TILE : (i + 1) * TILE]

    def operate(v, out_ref, c_out, up_ref, c_up, in_ref):
        vec[:, :p_slots] = two_parts(v)
        acc = [jnp.zeros((8, TILE), f32) for _ in range(2 * NT)]
        for k in range(1, 6):
            row, cand, _ = OFF[k]
            t = to_cols(NT + k, own(row))
            acc[cand] = acc[cand] + keep0[k] * t
            acc[cand + 1] = acc[cand + 1] + keep1[k] * t
        out_ref[...] = jnp.concatenate(acc[NT:], axis=1)
        when_start(has_up, c_out)
        for i in range(NT):
            acc[i] = acc[i] + to_rows(i, own(i))
        t = to_cols(NT, own(0))
        acc[1] = acc[1] + keep0[0] * t
        acc[2] = acc[2] + keep1[0] * t
        acc[0] = acc[0] + (keep0[0] + keep1[0]) * to_rows(NT, pick(vec, 0, True))
        when_recv(has_up, c_up)
        vec[:, p_slots:] = two_parts(up_ref[...])
        for k in range(1, 6):
            row = OFF[k][0]
            acc[row] = acc[row] + (keep0[k] + keep1[k]) * to_rows(NT + k, pick(vec, k, False))
        when_recv(has_down, c_out)
        total = jnp.concatenate(acc[:NT], axis=1) + in_ref[...]
        return v + strength * live * total

    def start_sums(first, second, part, got, ssem, rsem):
        part[0:8, :] = jnp.broadcast_to(jnp.sum(first, axis=1, keepdims=True), (8, 128))
        part[8:16, :] = jnp.broadcast_to(jnp.sum(second, axis=1, keepdims=True), (8, 128))
        copies = []
        for k in range(1, n):
            c = pltpu.make_async_remote_copy(
                src_ref=part, dst_ref=got.at[k - 1], send_sem=ssem.at[k - 1], recv_sem=rsem.at[k - 1],
                device_id={"pairs": lax.rem(me + k, n)}, device_id_type=mesh_ids,
            )
            c.start()
            copies.append(c)
        return copies

    def end_sums(copies, part, got):
        total = part[...]
        for k, c in enumerate(copies):
            c.wait_recv()
            total = total + got[k]
        return total[0:8, 0:1], total[8:16, 0:1]

    w = operate(r0, out1, c_1, up_r, c_r, in1)
    w_buf[...] = w
    when_start(has_down, c_w)
    sums1 = start_sums(r0 * r0, r0 * w, part1, got1, psend1, precv1)
    u = operate(w, out2, c_2, up_w, c_w, in2)
    norm0, curve0 = end_sums(sums1, part1, got1)
    step0 = norm0 / curve0
    r1 = r0 - step0 * w
    applied = w - step0 * u
    sums2 = start_sums(r1 * r1, r1 * applied, part2, got2, psend2, precv2)
    norm1, curve1 = end_sums(sums2, part2, got2)
    rescale = norm1 / norm0
    step1 = norm1 / (curve1 - rescale * norm1 / step0)
    sol_ref[...] = step0 * r0 + step1 * (r1 + rescale * r0)
    res_ref[...] = r1 - step1 * (applied + rescale * w)

    @pl.when(has_down)
    def _():
        for c in (*c_feat, c_r, c_w):
            c.wait_send()

    @pl.when(has_up)
    def _():
        for c in (c_1, c_2):
            c.wait_send()

    for c in sums1 + sums2:
        c.wait_send()


def on_device(n, features, inv_scale, cluster_order, counts, tile_cols, targets):
    p_slots = features.shape[1]
    rhs_rows = targets.shape[0]
    strength = 0.95 / (2 * BAND * TILE)
    padded = targets
    if rhs_rows < 8:
        padded = jnp.concatenate([targets, jnp.ones((8 - rhs_rows, p_slots), f32)], axis=0)
    vmem = pl.BlockSpec(memory_space=pltpu.VMEM)
    smem = pl.BlockSpec(memory_space=pltpu.SMEM)
    field = pltpu.VMEM((8, p_slots), f32)
    dma = pltpu.SemaphoreType.DMA
    tiles = 9
    out = jax.ShapeDtypeStruct((8, p_slots), f32)
    sol, res = pl.pallas_call(
        functools.partial(body, n, strength),
        out_shape=(out, out),
        in_specs=[vmem, vmem, vmem, smem, smem, vmem],
        out_specs=(vmem, vmem),
        scratch_shapes=[
            pltpu.VMEM((NT, FEAT, TILE), f32),
            pltpu.VMEM((NT, FEAT, TILE), f32),
            field, field, field, field, field, field, field, field,
            pltpu.VMEM((16, 128), f32),
            pltpu.VMEM((n - 1, 16, 128), f32),
            pltpu.VMEM((16, 128), f32),
            pltpu.VMEM((n - 1, 16, 128), f32),
            pltpu.VMEM((p_slots, DEPTH), bf16),
            pltpu.VMEM((DEPTH, 2 * p_slots), bf16),
            pltpu.VMEM((2, TILE, TILE), f32),
            pltpu.VMEM((tiles, TILE, TILE), bf16),
            pltpu.VMEM((tiles, TILE, TILE), bf16),
            pltpu.VMEM((16, 2 * p_slots), bf16),
            dma((7,)), dma((7,)),
            dma((n - 1,)), dma((n - 1,)), dma((n - 1,)), dma((n - 1,)),
        ],
        compiler_params=pltpu.CompilerParams(
            collective_id=0, has_side_effects=True, vmem_limit_bytes=48 * 2**20
        ),
    )(features, inv_scale[None, :], cluster_order[None, :], counts, tile_cols, padded)
    return sol[:rhs_rows], res[:rhs_rows]


def solution(mesh):
    return jax.shard_map(
        functools.partial(on_device, mesh.shape["pairs"]),
        mesh=mesh,
        in_specs=(
            P(None, ("groups", "pairs")),
            P(),
            P(("groups", "pairs")),
            P(("groups", "pairs")),
            P("groups", None),
            P("rhs", ("groups", "pairs")),
        ),
        out_specs=(P("rhs", ("groups", "pairs")), P("rhs", ("groups", "pairs"))),
        check_vma=False,
    )
```

```python
import functools
import math

import jax
import jax.numpy as jnp
from jax import lax
from jax.experimental import pallas as pl
from jax.experimental.pallas import tpu as pltpu
from jax.sharding import PartitionSpec as P

TILE = 512
BAND = 3
NT = 3
CHUNK = 64
LANES = 128
FEAT = 40
VMEM_ASK = 65_200_000
DEPTH = 256

root_three = math.sqrt(3.0)
log2_e = math.log2(math.e)
f32 = jnp.float32
bf16 = jnp.bfloat16

OFF = ((0, 1, 0), (0, 2, 1), (1, 2, 0), (1, 3, 1), (2, 3, 0), (2, 4, 1))


def three_parts(x):
    hi = x.astype(bf16).astype(f32)
    rest = x - hi
    mid = rest.astype(bf16).astype(f32)
    low = (rest - mid).astype(bf16).astype(f32)
    return hi, mid, low


def operand(x, is_row):
    hi, mid, low = three_parts(x)
    sq = jnp.sum(x * x, axis=0, keepdims=True)
    sq_hi, sq_mid, sq_low = three_parts(sq)
    width = x.shape[1]
    row = lax.broadcasted_iota(jnp.int32, (8, width), 0)
    first = 0 if is_row else 3
    tail = jnp.where(row < 6, 1.0, 0.0)
    tail = jnp.where(row == first, sq_hi, tail)
    tail = jnp.where(row == first + 1, sq_mid, tail)
    tail = jnp.where(row == first + 2, sq_low, tail)
    zero = jnp.zeros((8, width), f32)
    if is_row:
        parts = [-2.0 * y for y in (hi, hi, mid, hi, low, mid)]
    else:
        parts = [hi, mid, hi, low, hi, mid]
    return jnp.concatenate(parts + [tail, zero], axis=0)


def two_parts(v):
    hi = v.astype(bf16).astype(f32)
    return jnp.concatenate([hi, v - hi], axis=0).astype(bf16)


def fold(t):
    half = t.shape[0] // 2
    return t[:half] + t[half:]


def body(
    n, strength, raw_hbm, scale_ref, order_ref, counts_ref, cols_ref, targ_hbm, sol_ref, res_ref,
    raw_ref, targ_ref, load_sem, feat, up_feat, r_buf, up_r, w_buf, up_w, out1, in1, out2, in2, part1, got1, part2, got2,
    a_ref, b_ref, ds_ref, khi, klo, vec, send_sem, recv_sem, psend1, precv1, psend2, precv2,
):
    load_raw = pltpu.make_async_copy(raw_hbm, raw_ref, load_sem.at[0])
    load_targ = pltpu.make_async_copy(targ_hbm, targ_ref, load_sem.at[1])
    load_raw.start()
    load_targ.start()
    me = lax.axis_index("pairs")
    lane_rhs = lax.axis_index("rhs")
    mine = lax.rem(lane_rhs, 2)
    sibling = lane_rhs + 1 - 2 * mine
    mesh_ids = pl.DeviceIdType.MESH
    p_slots = NT * TILE
    has_up = me < n - 1
    has_down = me > 0

    barrier = pltpu.get_barrier_semaphore()
    for k in range(1, n):
        pl.semaphore_signal(barrier, inc=1, device_id={"pairs": lax.rem(me + k, n)}, device_id_type=mesh_ids)

    pl.semaphore_signal(barrier, inc=1, device_id={"rhs": sibling}, device_id_type=mesh_ids)

    lane = lax.broadcasted_iota(jnp.int32, (8, p_slots), 1)
    live = jnp.where(lane < counts_ref[0], 1.0, 0.0)

    @pl.when(jnp.logical_not(has_up))
    def _():
        up_feat[...] = jnp.zeros_like(up_feat)
        up_r[...] = jnp.zeros_like(up_r)
        up_w[...] = jnp.zeros_like(up_w)

    @pl.when(jnp.logical_not(has_down))
    def _():
        in1[...] = jnp.zeros_like(in1)
        in2[...] = jnp.zeros_like(in2)

    diag = lax.broadcasted_iota(jnp.int32, (FEAT, FEAT), 0) == lax.broadcasted_iota(jnp.int32, (FEAT, FEAT), 1)
    scale = jnp.sum(jnp.where(diag, jnp.broadcast_to(scale_ref[...], (FEAT, FEAT)), 0.0), axis=1, keepdims=True)

    def gather_tile(i):
        for c in range(TILE // LANES):
            first = i * TILE + c * LANES
            index = order_ref[first // LANES : first // LANES + 1, :] - me * p_slots
            index = jnp.broadcast_to(index, (FEAT, LANES))
            group = lax.shift_right_logical(index, 7)
            within = jnp.bitwise_and(index, LANES - 1)
            got = jnp.zeros((FEAT, LANES), f32)
            for s in range(p_slots // LANES):
                part = jnp.take_along_axis(raw_ref[:, s * LANES : (s + 1) * LANES], within, axis=1)
                got = jnp.where(group == s, part, got)
            feat[i, c // 2, :, c % 2 * LANES : (c % 2 + 1) * LANES] = got * scale

    load_raw.wait()
    gather_tile(0)
    pl.semaphore_wait(barrier, n)

    def shift(src, dst, slot, by):
        return pltpu.make_async_remote_copy(
            src_ref=src, dst_ref=dst, send_sem=send_sem.at[slot], recv_sem=recv_sem.at[slot],
            device_id={"pairs": lax.rem(me + by + n, n)}, device_id_type=mesh_ids,
        )

    c_feat = [shift(feat.at[i, mine], up_feat.at[i, mine], 4 + i, -1) for i in range(NT)]
    c_hand = [
        pltpu.make_async_remote_copy(
            src_ref=up_feat.at[i, mine], dst_ref=up_feat.at[i, mine],
            send_sem=send_sem.at[7 + i], recv_sem=recv_sem.at[7 + i],
            device_id={"rhs": sibling}, device_id_type=mesh_ids,
        )
        for i in range(NT)
    ]

    def hand_on(i):
        @pl.when(has_up)
        def _():
            c_feat[i].wait_recv()
            c_hand[i].start()

    c_r = shift(r_buf, up_r, 0, -1)
    c_w = shift(w_buf, up_w, 1, -1)
    c_1 = shift(out1, in1, 2, 1)
    c_2 = shift(out2, in2, 3, 1)

    def when_start(cond, *copies):
        @pl.when(cond)
        def _():
            for c in copies:
                c.start()

    def when_recv(cond, *copies):
        @pl.when(cond)
        def _():
            for c in copies:
                c.wait_recv()

    when_start(has_down, c_feat[0])
    gather_tile(1)
    when_start(has_down, c_feat[1])
    gather_tile(2)
    load_targ.wait()
    r0 = targ_ref[...] * live
    r_buf[...] = r0
    when_start(has_down, c_feat[2], c_r)

    base = me * NT
    start, keep0, keep1 = [], [], []
    for row, cand, slot in OFF:
        a = cols_ref[base + row, 1]
        b = cols_ref[base + row, 2]
        a_in = jnp.where(a < 0, row + 3, a - base)
        b_in = jnp.where(b < 0, row + 3, b - base)
        if slot == 0:
            valid = jnp.maximum(a, b) >= 0
            c = jnp.minimum(jnp.minimum(a_in, b_in), cand + 1)
        else:
            valid = jnp.minimum(a, b) >= 0
            c = jnp.maximum(a_in, b_in)
        start.append(c)
        keep0.append(jnp.where(valid & (c == cand), 1.0, 0.0).astype(f32))
        keep1.append(jnp.where(valid & (c == cand + 1), 1.0, 0.0).astype(f32))

    def pick(ref, k, own):
        cand = OFF[k][1]
        lo = ref[:, cand * TILE : (cand + 1) * TILE]
        hi = ref[:, (cand + 1) * TILE : (cand + 2) * TILE]
        return jnp.where(start[k] == cand, lo, hi)

    for i in range(NT):
        span = slice(i * TILE, (i + 1) * TILE)
        x = jnp.concatenate([feat[i, 0], feat[i, 1]], axis=1)
        a_ref[span, :] = operand(x, True).T.astype(bf16)
        b_ref[:, span] = operand(x, False).astype(bf16)

    def form(t, row, cols):
        ds_ref[t % 2] = jnp.dot(a_ref[row * TILE : (row + 1) * TILE, :], cols, preferred_element_type=f32)
        for s in range(TILE // CHUNK):
            at = slice(s * CHUNK, (s + 1) * CHUNK)
            d2 = jnp.maximum(ds_ref[t % 2, at, :], 0.0) + 1e-6
            d = d2 * lax.rsqrt(d2)
            env = jnp.maximum(1.0 - d, 0.0)
            k = (1.0 + root_three * d) * jnp.exp2((-root_three * log2_e) * d) * (env * env)
            hi = k.astype(bf16)
            khi[t, at, :] = hi
            klo[t, at, :] = (k - hi.astype(f32)).astype(bf16)

    nt_dims = (((1,), (1,)), ((), ()))

    def to_rows(t, v):
        return fold(
            lax.dot_general(v, khi[t], nt_dims, preferred_element_type=f32)
            + lax.dot_general(v, klo[t], nt_dims, preferred_element_type=f32)
        )

    def to_cols(t, v):
        return fold(
            jnp.dot(v, khi[t], preferred_element_type=f32)
            + jnp.dot(v, klo[t], preferred_element_type=f32)
        )

    for i in range(NT):
        form(i, i, b_ref[:, i * TILE : (i + 1) * TILE])
    hand_on(0)
    form(NT, 0, pick(b_ref, 0, True))
    hand_on(1)
    for i, pairs in ((0, (1, 2)), (1, (3, 4)), (2, (5,))):
        when_recv(has_up, c_hand[i])
        up_x = jnp.concatenate([up_feat[i, 0], up_feat[i, 1]], axis=1)
        b_ref[:, p_slots + i * TILE : p_slots + (i + 1) * TILE] = operand(up_x, False).astype(bf16)
        for k in pairs:
            form(NT + k, OFF[k][0], pick(b_ref, k, False))
        if i == 0:
            hand_on(2)

    def own(i):
        return vec[:, i * TILE : (i + 1) * TILE]

    def operate(v, out_ref, c_out, up_ref, c_up, in_ref):
        vec[:, :p_slots] = two_parts(v)
        acc = [jnp.zeros((8, TILE), f32) for _ in range(2 * NT)]
        for k in range(1, 6):
            row, cand, _ = OFF[k]
            t = to_cols(NT + k, own(row))
            acc[cand] = acc[cand] + keep0[k] * t
            acc[cand + 1] = acc[cand + 1] + keep1[k] * t
        out_ref[...] = jnp.concatenate(acc[NT:], axis=1)
        when_start(has_up, c_out)
        for i in range(NT):
            acc[i] = acc[i] + to_rows(i, own(i))
        t = to_cols(NT, own(0))
        acc[1] = acc[1] + keep0[0] * t
        acc[2] = acc[2] + keep1[0] * t
        acc[0] = acc[0] + (keep0[0] + keep1[0]) * to_rows(NT, pick(vec, 0, True))
        when_recv(has_up, c_up)
        vec[:, p_slots:] = two_parts(up_ref[...])
        for k in range(1, 6):
            row = OFF[k][0]
            acc[row] = acc[row] + (keep0[k] + keep1[k]) * to_rows(NT + k, pick(vec, k, False))
        when_recv(has_down, c_out)
        total = jnp.concatenate(acc[:NT], axis=1) + in_ref[...]
        return v + strength * live * total

    def start_sums(first, second, part, got, ssem, rsem):
        part[0:8, :] = jnp.broadcast_to(jnp.sum(first, axis=1, keepdims=True), (8, 128))
        part[8:16, :] = jnp.broadcast_to(jnp.sum(second, axis=1, keepdims=True), (8, 128))
        copies = []
        for k in range(1, n):
            c = pltpu.make_async_remote_copy(
                src_ref=part, dst_ref=got.at[k - 1], send_sem=ssem.at[k - 1], recv_sem=rsem.at[k - 1],
                device_id={"pairs": lax.rem(me + k, n)}, device_id_type=mesh_ids,
            )
            c.start()
            copies.append(c)
        return copies

    def end_sums(copies, part, got):
        total = part[...]
        for k, c in enumerate(copies):
            c.wait_recv()
            total = total + got[k]
        return total[0:8, 0:1], total[8:16, 0:1]

    w = operate(r0, out1, c_1, up_r, c_r, in1)
    w_buf[...] = w
    when_start(has_down, c_w)
    sums1 = start_sums(r0 * r0, r0 * w, part1, got1, psend1, precv1)
    u = operate(w, out2, c_2, up_w, c_w, in2)
    norm0, curve0 = end_sums(sums1, part1, got1)
    step0 = norm0 / curve0
    r1 = r0 - step0 * w
    applied = w - step0 * u
    sums2 = start_sums(r1 * r1, r1 * applied, part2, got2, psend2, precv2)
    norm1, curve1 = end_sums(sums2, part2, got2)
    rescale = norm1 / norm0
    step1 = norm1 / (curve1 - rescale * norm1 / step0)
    sol_ref[...] = step0 * r0 + step1 * (r1 + rescale * r0)
    res_ref[...] = r1 - step1 * (applied + rescale * w)

    @pl.when(has_down)
    def _():
        for c in (*c_feat, c_r, c_w):
            c.wait_send()

    @pl.when(has_up)
    def _():
        for c in (c_1, c_2, *c_hand):
            c.wait_send()

    for c in sums1 + sums2:
        c.wait_send()


def on_device(n, features, inv_scale, cluster_order, counts, tile_cols, targets):
    p_slots = features.shape[1]
    rhs_rows = targets.shape[0]
    strength = 0.95 / (2 * BAND * TILE)
    padded = targets
    if rhs_rows < 8:
        padded = jnp.concatenate([targets, jnp.ones((8 - rhs_rows, p_slots), f32)], axis=0)
    vmem = pl.BlockSpec(memory_space=pltpu.VMEM)
    hbm = pl.BlockSpec(memory_space=pltpu.HBM)
    smem = pl.BlockSpec(memory_space=pltpu.SMEM)
    field = pltpu.VMEM((8, p_slots), f32)
    dma = pltpu.SemaphoreType.DMA
    tiles = 9
    out = jax.ShapeDtypeStruct((8, p_slots), f32)
    sol, res = pl.pallas_call(
        functools.partial(body, n, strength),
        out_shape=(out, out),
        in_specs=[hbm, vmem, vmem, smem, smem, hbm],
        out_specs=(vmem, vmem),
        scratch_shapes=[
            pltpu.VMEM((FEAT, p_slots), f32),
            field,
            dma((2,)),
            pltpu.VMEM((NT, 2, FEAT, TILE // 2), f32),
            pltpu.VMEM((NT, 2, FEAT, TILE // 2), f32),
            field, field, field, field, field, field, field, field,
            pltpu.VMEM((16, 128), f32),
            pltpu.VMEM((n - 1, 16, 128), f32),
            pltpu.VMEM((16, 128), f32),
            pltpu.VMEM((n - 1, 16, 128), f32),
            pltpu.VMEM((p_slots, DEPTH), bf16),
            pltpu.VMEM((DEPTH, 2 * p_slots), bf16),
            pltpu.VMEM((2, TILE, TILE), f32),
            pltpu.VMEM((tiles, TILE, TILE), bf16),
            pltpu.VMEM((tiles, TILE, TILE), bf16),
            pltpu.VMEM((16, 2 * p_slots), bf16),
            dma((10,)), dma((10,)),
            dma((n - 1,)), dma((n - 1,)), dma((n - 1,)), dma((n - 1,)),
        ],
        compiler_params=pltpu.CompilerParams(
            collective_id=0, has_side_effects=True, vmem_limit_bytes=VMEM_ASK
        ),
    )(features, inv_scale[None, :], cluster_order.reshape(p_slots // LANES, LANES), counts, tile_cols, padded)
    return sol[:rhs_rows], res[:rhs_rows]


def solution(mesh):
    return jax.shard_map(
        functools.partial(on_device, mesh.shape["pairs"]),
        mesh=mesh,
        in_specs=(
            P(None, ("groups", "pairs")),
            P(),
            P(("groups", "pairs")),
            P(("groups", "pairs")),
            P("groups", None),
            P("rhs", ("groups", "pairs")),
        ),
        out_specs=(P("rhs", ("groups", "pairs")), P("rhs", ("groups", "pairs"))),
        check_vma=False,
    )
```

```python
import functools
import math

import jax
import jax.numpy as jnp
from jax import lax
from jax.experimental import pallas as pl
from jax.experimental.pallas import tpu as pltpu
from jax.sharding import PartitionSpec as P

TILE = 512
BAND = 3
NT = 3
CHUNK = 64
LANES = 128
FEAT = 40
VMEM_ASK = 65_100_000
DEPTH = 256

root_three = math.sqrt(3.0)
log2_e = math.log2(math.e)
f32 = jnp.float32
bf16 = jnp.bfloat16

OFF = ((0, 1, 0), (0, 2, 1), (1, 2, 0), (1, 3, 1), (2, 3, 0), (2, 4, 1))


def three_parts(x):
    hi = x.astype(bf16).astype(f32)
    rest = x - hi
    mid = rest.astype(bf16).astype(f32)
    low = (rest - mid).astype(bf16).astype(f32)
    return hi, mid, low


def operand(x, is_row):
    hi, mid, low = three_parts(x)
    sq = jnp.sum(x * x, axis=0, keepdims=True)
    sq_hi, sq_mid, sq_low = three_parts(sq)
    width = x.shape[1]
    row = lax.broadcasted_iota(jnp.int32, (8, width), 0)
    first = 0 if is_row else 3
    tail = jnp.where(row < 6, 1.0, 0.0)
    tail = jnp.where(row == first, sq_hi, tail)
    tail = jnp.where(row == first + 1, sq_mid, tail)
    tail = jnp.where(row == first + 2, sq_low, tail)
    zero = jnp.zeros((8, width), f32)
    if is_row:
        parts = [-2.0 * y for y in (hi, hi, mid, hi, low, mid)]
    else:
        parts = [hi, mid, hi, low, hi, mid]
    return jnp.concatenate(parts + [tail, zero], axis=0)


def two_parts(v):
    hi = v.astype(bf16).astype(f32)
    return jnp.concatenate([hi, v - hi], axis=0).astype(bf16)


def fold(t):
    half = t.shape[0] // 2
    return t[:half] + t[half:]


def body(
    n, strength, raw_hbm, scale_ref, order_ref, counts_ref, cols_ref, targ_hbm, sol_ref, res_ref,
    raw_ref, targ_ref, load_sem, feat, up_feat, r_buf, up_r, w_buf, up_w, out1, in1, out2, in2, part1, got1, part2, got2,
    a_ref, b_ref, ds_ref, khi, klo, vec, tall, send_sem, recv_sem, psend1, precv1, psend2, precv2,
):
    load_raw = pltpu.make_async_copy(raw_hbm, raw_ref, load_sem.at[0])
    load_targ = pltpu.make_async_copy(targ_hbm, targ_ref, load_sem.at[1])
    load_raw.start()
    load_targ.start()
    me = lax.axis_index("pairs")
    lane_rhs = lax.axis_index("rhs")
    mine = lax.rem(lane_rhs, 2)
    sibling = lane_rhs + 1 - 2 * mine
    mesh_ids = pl.DeviceIdType.MESH
    p_slots = NT * TILE
    has_up = me < n - 1
    has_down = me > 0

    barrier = pltpu.get_barrier_semaphore()
    for k in range(1, n):
        pl.semaphore_signal(barrier, inc=1, device_id={"pairs": lax.rem(me + k, n)}, device_id_type=mesh_ids)

    pl.semaphore_signal(barrier, inc=1, device_id={"rhs": sibling}, device_id_type=mesh_ids)

    lane = lax.broadcasted_iota(jnp.int32, (8, p_slots), 1)
    live = jnp.where(lane < counts_ref[0], 1.0, 0.0)

    @pl.when(jnp.logical_not(has_up))
    def _():
        up_feat[...] = jnp.zeros_like(up_feat)
        up_r[...] = jnp.zeros_like(up_r)
        up_w[...] = jnp.zeros_like(up_w)

    @pl.when(jnp.logical_not(has_down))
    def _():
        in1[...] = jnp.zeros_like(in1)
        in2[...] = jnp.zeros_like(in2)

    diag = lax.broadcasted_iota(jnp.int32, (FEAT, FEAT), 0) == lax.broadcasted_iota(jnp.int32, (FEAT, FEAT), 1)
    scale = jnp.sum(jnp.where(diag, jnp.broadcast_to(scale_ref[...], (FEAT, FEAT)), 0.0), axis=1, keepdims=True)

    def gather_tile(i):
        for c in range(TILE // LANES):
            first = i * TILE + c * LANES
            index = order_ref[first // LANES : first // LANES + 1, :] - me * p_slots
            index = jnp.broadcast_to(index, (FEAT, LANES))
            group = lax.shift_right_logical(index, 7)
            within = jnp.bitwise_and(index, LANES - 1)
            got = jnp.zeros((FEAT, LANES), f32)
            for s in range(p_slots // LANES):
                part = jnp.take_along_axis(raw_ref[:, s * LANES : (s + 1) * LANES], within, axis=1)
                got = jnp.where(group == s, part, got)
            feat[i, c // 2, :, c % 2 * LANES : (c % 2 + 1) * LANES] = got * scale

    load_raw.wait()
    gather_tile(0)
    pl.semaphore_wait(barrier, n)

    def shift(src, dst, slot, by):
        return pltpu.make_async_remote_copy(
            src_ref=src, dst_ref=dst, send_sem=send_sem.at[slot], recv_sem=recv_sem.at[slot],
            device_id={"pairs": lax.rem(me + by + n, n)}, device_id_type=mesh_ids,
        )

    c_feat = [shift(feat.at[i, mine], up_feat.at[i, mine], 4 + i, -1) for i in range(NT)]
    c_hand = [
        pltpu.make_async_remote_copy(
            src_ref=up_feat.at[i, mine], dst_ref=up_feat.at[i, mine],
            send_sem=send_sem.at[7 + i], recv_sem=recv_sem.at[7 + i],
            device_id={"rhs": sibling}, device_id_type=mesh_ids,
        )
        for i in range(NT)
    ]

    def hand_on(i):
        @pl.when(has_up)
        def _():
            c_feat[i].wait_recv()
            c_hand[i].start()

    c_r = shift(r_buf, up_r, 0, -1)
    c_w = shift(w_buf, up_w, 1, -1)
    c_1 = shift(out1, in1, 2, 1)
    c_2 = shift(out2, in2, 3, 1)

    def when_start(cond, *copies):
        @pl.when(cond)
        def _():
            for c in copies:
                c.start()

    def when_recv(cond, *copies):
        @pl.when(cond)
        def _():
            for c in copies:
                c.wait_recv()

    when_start(has_down, c_feat[0])
    gather_tile(1)
    when_start(has_down, c_feat[1])
    gather_tile(2)
    load_targ.wait()
    r0 = targ_ref[...] * live
    r_buf[...] = r0
    when_start(has_down, c_feat[2], c_r)

    base = me * NT
    start, keep0, keep1 = [], [], []
    for row, cand, slot in OFF:
        a = cols_ref[1, base + row]
        b = cols_ref[2, base + row]
        a_in = jnp.where(a < 0, row + 3, a - base)
        b_in = jnp.where(b < 0, row + 3, b - base)
        if slot == 0:
            valid = jnp.maximum(a, b) >= 0
            c = jnp.minimum(jnp.minimum(a_in, b_in), cand + 1)
        else:
            valid = jnp.minimum(a, b) >= 0
            c = jnp.maximum(a_in, b_in)
        start.append(c)
        keep0.append(jnp.where(valid & (c == cand), 1.0, 0.0).astype(f32))
        keep1.append(jnp.where(valid & (c == cand + 1), 1.0, 0.0).astype(f32))

    def pick(ref, k, own):
        cand = OFF[k][1]
        lo = ref[:, cand * TILE : (cand + 1) * TILE]
        hi = ref[:, (cand + 1) * TILE : (cand + 2) * TILE]
        return jnp.where(start[k] == cand, lo, hi)

    for i in range(NT):
        span = slice(i * TILE, (i + 1) * TILE)
        x = jnp.concatenate([feat[i, 0], feat[i, 1]], axis=1)
        a_ref[span, :] = operand(x, True).T.astype(bf16)
        b_ref[:, span] = operand(x, False).astype(bf16)

    def form(t, row, cols):
        ds_ref[t % 2] = jnp.dot(a_ref[row * TILE : (row + 1) * TILE, :], cols, preferred_element_type=f32)
        for s in range(TILE // CHUNK):
            at = slice(s * CHUNK, (s + 1) * CHUNK)
            d2 = jnp.maximum(ds_ref[t % 2, at, :], 0.0) + 1e-6
            d = d2 * lax.rsqrt(d2)
            env = jnp.maximum(1.0 - d, 0.0)
            k = (1.0 + root_three * d) * jnp.exp2((-root_three * log2_e) * d) * (env * env)
            hi = k.astype(bf16)
            khi[t, at, :] = hi
            klo[t, at, :] = (k - hi.astype(f32)).astype(bf16)

    def to_rows(t, v):
        return jnp.dot(khi[t], v, preferred_element_type=f32) + jnp.dot(klo[t], v, preferred_element_type=f32)

    def upright(v):
        parts = two_parts(v).astype(f32)
        wide = jnp.concatenate([parts, jnp.zeros((LANES - 16, p_slots), f32)], axis=0)
        return wide.T.astype(bf16)

    def pick_rows(k):
        cand = OFF[k][1]
        lo = tall[cand * TILE : (cand + 1) * TILE, :]
        hi = tall[(cand + 1) * TILE : (cand + 2) * TILE, :]
        return jnp.where(start[k] == cand, lo, hi)

    def to_cols(t, v):
        return fold(
            jnp.dot(v, khi[t], preferred_element_type=f32)
            + jnp.dot(v, klo[t], preferred_element_type=f32)
        )

    for i in range(NT):
        form(i, i, b_ref[:, i * TILE : (i + 1) * TILE])
    hand_on(0)
    form(NT, 0, pick(b_ref, 0, True))
    hand_on(1)
    for i, pairs in ((0, (1, 2)), (1, (3, 4)), (2, (5,))):
        when_recv(has_up, c_hand[i])
        up_x = jnp.concatenate([up_feat[i, 0], up_feat[i, 1]], axis=1)
        b_ref[:, p_slots + i * TILE : p_slots + (i + 1) * TILE] = operand(up_x, False).astype(bf16)
        for k in pairs:
            form(NT + k, OFF[k][0], pick(b_ref, k, False))
        if i == 0:
            hand_on(2)

    def own(i):
        return vec[:, i * TILE : (i + 1) * TILE]

    def operate(v, out_ref, c_out, up_ref, c_up, in_ref):
        vec[:, :p_slots] = two_parts(v)
        tall[:p_slots, :] = upright(v)
        acc = [jnp.zeros((8, TILE), f32) for _ in range(2 * NT)]
        for k in range(1, 6):
            row, cand, _ = OFF[k]
            t = to_cols(NT + k, own(row))
            acc[cand] = acc[cand] + keep0[k] * t
            acc[cand + 1] = acc[cand + 1] + keep1[k] * t
        out_ref[...] = jnp.concatenate(acc[NT:], axis=1)
        when_start(has_up, c_out)
        for i in range(NT):
            acc[i] = acc[i] + to_cols(i, own(i))
        t = to_cols(NT, own(0))
        acc[1] = acc[1] + keep0[0] * t
        acc[2] = acc[2] + keep1[0] * t
        side = [(keep0[0] + keep1[0]) * to_rows(NT, pick_rows(0)), None, None]
        when_recv(has_up, c_up)
        tall[p_slots:, :] = upright(up_ref[...])
        for k in range(1, 6):
            row = OFF[k][0]
            t = (keep0[k] + keep1[k]) * to_rows(NT + k, pick_rows(k))
            side[row] = t if side[row] is None else side[row] + t
        for row in range(NT):
            acc[row] = acc[row] + fold(side[row].T[:16])
        when_recv(has_down, c_out)
        total = jnp.concatenate(acc[:NT], axis=1) + in_ref[...]
        return v + strength * live * total

    def start_sums(first, second, part, got, ssem, rsem):
        part[0:8, :] = jnp.broadcast_to(jnp.sum(first, axis=1, keepdims=True), (8, 128))
        part[8:16, :] = jnp.broadcast_to(jnp.sum(second, axis=1, keepdims=True), (8, 128))
        copies = []
        for k in range(1, n):
            c = pltpu.make_async_remote_copy(
                src_ref=part, dst_ref=got.at[k - 1], send_sem=ssem.at[k - 1], recv_sem=rsem.at[k - 1],
                device_id={"pairs": lax.rem(me + k, n)}, device_id_type=mesh_ids,
            )
            c.start()
            copies.append(c)
        return copies

    def end_sums(copies, part, got):
        total = part[...]
        for k, c in enumerate(copies):
            c.wait_recv()
            total = total + got[k]
        return total[0:8, 0:1], total[8:16, 0:1]

    w = operate(r0, out1, c_1, up_r, c_r, in1)
    w_buf[...] = w
    when_start(has_down, c_w)
    sums1 = start_sums(r0 * r0, r0 * w, part1, got1, psend1, precv1)
    u = operate(w, out2, c_2, up_w, c_w, in2)
    norm0, curve0 = end_sums(sums1, part1, got1)
    step0 = norm0 / curve0
    r1 = r0 - step0 * w
    applied = w - step0 * u
    sums2 = start_sums(r1 * r1, r1 * applied, part2, got2, psend2, precv2)
    norm1, curve1 = end_sums(sums2, part2, got2)
    rescale = norm1 / norm0
    step1 = norm1 / (curve1 - rescale * norm1 / step0)
    sol_ref[...] = step0 * r0 + step1 * (r1 + rescale * r0)
    res_ref[...] = r1 - step1 * (applied + rescale * w)

    @pl.when(has_down)
    def _():
        for c in (*c_feat, c_r, c_w):
            c.wait_send()

    @pl.when(has_up)
    def _():
        for c in (c_1, c_2, *c_hand):
            c.wait_send()

    for c in sums1 + sums2:
        c.wait_send()


def on_device(n, features, inv_scale, cluster_order, counts, tile_cols, targets):
    p_slots = features.shape[1]
    rhs_rows = targets.shape[0]
    strength = 0.95 / (2 * BAND * TILE)
    padded = targets
    if rhs_rows < 8:
        padded = jnp.concatenate([targets, jnp.ones((8 - rhs_rows, p_slots), f32)], axis=0)
    vmem = pl.BlockSpec(memory_space=pltpu.VMEM)
    hbm = pl.BlockSpec(memory_space=pltpu.HBM)
    smem = pl.BlockSpec(memory_space=pltpu.SMEM)
    field = pltpu.VMEM((8, p_slots), f32)
    dma = pltpu.SemaphoreType.DMA
    tiles = 9
    out = jax.ShapeDtypeStruct((8, p_slots), f32)
    sol, res = pl.pallas_call(
        functools.partial(body, n, strength),
        out_shape=(out, out),
        in_specs=[hbm, vmem, vmem, smem, smem, hbm],
        out_specs=(vmem, vmem),
        scratch_shapes=[
            pltpu.VMEM((FEAT, p_slots), f32),
            field,
            dma((2,)),
            pltpu.VMEM((NT, 2, FEAT, TILE // 2), f32),
            pltpu.VMEM((NT, 2, FEAT, TILE // 2), f32),
            field, field, field, field, field, field, field, field,
            pltpu.VMEM((16, 128), f32),
            pltpu.VMEM((n - 1, 16, 128), f32),
            pltpu.VMEM((16, 128), f32),
            pltpu.VMEM((n - 1, 16, 128), f32),
            pltpu.VMEM((p_slots, DEPTH), bf16),
            pltpu.VMEM((DEPTH, 2 * p_slots), bf16),
            pltpu.VMEM((2, TILE, TILE), f32),
            pltpu.VMEM((tiles, TILE, TILE), bf16),
            pltpu.VMEM((tiles, TILE, TILE), bf16),
            pltpu.VMEM((16, p_slots), bf16),
            pltpu.VMEM((2 * p_slots, LANES), bf16),
            dma((10,)), dma((10,)),
            dma((n - 1,)), dma((n - 1,)), dma((n - 1,)), dma((n - 1,)),
        ],
        compiler_params=pltpu.CompilerParams(
            collective_id=0, has_side_effects=True, vmem_limit_bytes=VMEM_ASK
        ),
    )(features, inv_scale[None, :], cluster_order.reshape(p_slots // LANES, LANES), counts, tile_cols.T, padded)
    return sol[:rhs_rows], res[:rhs_rows]


def solution(mesh):
    return jax.shard_map(
        functools.partial(on_device, mesh.shape["pairs"]),
        mesh=mesh,
        in_specs=(
            P(None, ("groups", "pairs")),
            P(),
            P(("groups", "pairs")),
            P(("groups", "pairs")),
            P("groups", None),
            P("rhs", ("groups", "pairs")),
        ),
        out_specs=(P("rhs", ("groups", "pairs")), P("rhs", ("groups", "pairs"))),
        check_vma=False,
    )
```

```python
import functools
import math

import jax
import jax.numpy as jnp
from jax import lax
from jax.experimental import pallas as pl
from jax.experimental.pallas import tpu as pltpu
from jax.sharding import PartitionSpec as P

TILE = 512
BAND = 3
NT = 3
CHUNK = 64
LANES = 128
FEAT = 40
VMEM_ASK = 64_980_000
DEPTH = 256

root_three = math.sqrt(3.0)
log2_e = math.log2(math.e)
f32 = jnp.float32
bf16 = jnp.bfloat16

OFF = ((0, 1, 0), (0, 2, 1), (1, 2, 0), (1, 3, 1), (2, 3, 0), (2, 4, 1))


def three_parts(x):
    hi = x.astype(bf16).astype(f32)
    rest = x - hi
    mid = rest.astype(bf16).astype(f32)
    low = (rest - mid).astype(bf16).astype(f32)
    return hi, mid, low


def operand(x, is_row):
    hi, mid, low = three_parts(x)
    sq = jnp.sum(x * x, axis=0, keepdims=True)
    sq_hi, sq_mid, sq_low = three_parts(sq)
    width = x.shape[1]
    row = lax.broadcasted_iota(jnp.int32, (8, width), 0)
    first = 0 if is_row else 3
    tail = jnp.where(row < 6, 1.0, 0.0)
    tail = jnp.where(row == first, sq_hi, tail)
    tail = jnp.where(row == first + 1, sq_mid, tail)
    tail = jnp.where(row == first + 2, sq_low, tail)
    zero = jnp.zeros((8, width), f32)
    if is_row:
        parts = [-2.0 * y for y in (hi, hi, mid, hi, low, mid)]
    else:
        parts = [hi, mid, hi, low, hi, mid]
    return jnp.concatenate(parts + [tail, zero], axis=0)


def two_parts(v):
    hi = v.astype(bf16).astype(f32)
    return jnp.concatenate([hi, v - hi], axis=0).astype(bf16)


def fold(t):
    half = t.shape[0] // 2
    return t[:half] + t[half:]


def body(
    n, strength, raw_hbm, scale_ref, order_ref, counts_ref, cols_ref, targ_hbm, sol_ref, res_ref,
    raw_ref, targ_ref, load_sem, feat, up_feat, r_buf, up_r, w_buf, up_w, out1, in1, out2, in2, part1, got1, part2, got2,
    a_ref, b_ref, ds_ref, khi, klo, vec, tall, send_sem, recv_sem, psend1, precv1, psend2, precv2,
):
    load_raw = pltpu.make_async_copy(raw_hbm, raw_ref, load_sem.at[0])
    load_targ = pltpu.make_async_copy(targ_hbm, targ_ref, load_sem.at[1])
    load_raw.start()
    load_targ.start()
    me = lax.axis_index("pairs")
    lane_rhs = lax.axis_index("rhs")
    mine = lax.rem(lane_rhs, 2)
    sibling = lane_rhs + 1 - 2 * mine
    mesh_ids = pl.DeviceIdType.MESH
    p_slots = NT * TILE
    has_up = me < n - 1
    has_down = me > 0

    barrier = pltpu.get_barrier_semaphore()
    for k in range(1, n):
        pl.semaphore_signal(barrier, inc=1, device_id={"pairs": lax.rem(me + k, n)}, device_id_type=mesh_ids)

    pl.semaphore_signal(barrier, inc=1, device_id={"rhs": sibling}, device_id_type=mesh_ids)

    lane = lax.broadcasted_iota(jnp.int32, (8, p_slots), 1)
    live = jnp.where(lane < counts_ref[0], 1.0, 0.0)

    @pl.when(jnp.logical_not(has_up))
    def _():
        up_feat[...] = jnp.zeros_like(up_feat)
        up_r[...] = jnp.zeros_like(up_r)
        up_w[...] = jnp.zeros_like(up_w)

    @pl.when(jnp.logical_not(has_down))
    def _():
        in1[...] = jnp.zeros_like(in1)
        in2[...] = jnp.zeros_like(in2)

    diag = lax.broadcasted_iota(jnp.int32, (FEAT, FEAT), 0) == lax.broadcasted_iota(jnp.int32, (FEAT, FEAT), 1)
    scale = jnp.sum(jnp.where(diag, jnp.broadcast_to(scale_ref[...], (FEAT, FEAT)), 0.0), axis=1, keepdims=True)

    def gather_tile(i):
        for c in range(TILE // LANES):
            first = i * TILE + c * LANES
            index = order_ref[first // LANES : first // LANES + 1, :] - me * p_slots
            index = jnp.broadcast_to(index, (FEAT, LANES))
            group = lax.shift_right_logical(index, 7)
            within = jnp.bitwise_and(index, LANES - 1)
            got = jnp.zeros((FEAT, LANES), f32)
            for s in range(p_slots // LANES):
                part = jnp.take_along_axis(raw_ref[:, s * LANES : (s + 1) * LANES], within, axis=1)
                got = jnp.where(group == s, part, got)
            feat[i, c // 2, :, c % 2 * LANES : (c % 2 + 1) * LANES] = got * scale

    load_raw.wait()
    gather_tile(0)
    pl.semaphore_wait(barrier, n)

    def shift(src, dst, slot, by):
        return pltpu.make_async_remote_copy(
            src_ref=src, dst_ref=dst, send_sem=send_sem.at[slot], recv_sem=recv_sem.at[slot],
            device_id={"pairs": lax.rem(me + by + n, n)}, device_id_type=mesh_ids,
        )

    c_feat = [shift(feat.at[i, mine], up_feat.at[i, mine], 4 + i, -1) for i in range(NT)]
    c_hand = [
        pltpu.make_async_remote_copy(
            src_ref=up_feat.at[i, mine], dst_ref=up_feat.at[i, mine],
            send_sem=send_sem.at[7 + i], recv_sem=recv_sem.at[7 + i],
            device_id={"rhs": sibling}, device_id_type=mesh_ids,
        )
        for i in range(NT)
    ]

    def hand_on(i):
        @pl.when(has_up)
        def _():
            c_feat[i].wait_recv()
            c_hand[i].start()

    c_r = shift(r_buf, up_r, 0, -1)
    c_w = shift(w_buf, up_w, 1, -1)
    c_1 = shift(out1, in1, 2, 1)
    c_2 = shift(out2, in2, 3, 1)

    def when_start(cond, *copies):
        @pl.when(cond)
        def _():
            for c in copies:
                c.start()

    def when_recv(cond, *copies):
        @pl.when(cond)
        def _():
            for c in copies:
                c.wait_recv()

    when_start(has_down, c_feat[0])
    gather_tile(1)
    when_start(has_down, c_feat[1])
    gather_tile(2)
    load_targ.wait()
    r0 = targ_ref[...] * live
    r_buf[...] = r0
    when_start(has_down, c_feat[2], c_r)

    base = me * NT
    start, keep0, keep1 = [], [], []
    for row, cand, slot in OFF:
        a = cols_ref[1, base + row]
        b = cols_ref[2, base + row]
        a_in = jnp.where(a < 0, row + 3, a - base)
        b_in = jnp.where(b < 0, row + 3, b - base)
        if slot == 0:
            valid = jnp.maximum(a, b) >= 0
            c = jnp.minimum(jnp.minimum(a_in, b_in), cand + 1)
        else:
            valid = jnp.minimum(a, b) >= 0
            c = jnp.maximum(a_in, b_in)
        start.append(c)
        keep0.append(jnp.where(valid & (c == cand), 1.0, 0.0).astype(f32))
        keep1.append(jnp.where(valid & (c == cand + 1), 1.0, 0.0).astype(f32))

    def pick(ref, k, own):
        cand = OFF[k][1]
        lo = ref[:, cand * TILE : (cand + 1) * TILE]
        hi = ref[:, (cand + 1) * TILE : (cand + 2) * TILE]
        return jnp.where(start[k] == cand, lo, hi)

    for i in range(NT):
        span = slice(i * TILE, (i + 1) * TILE)
        x = jnp.concatenate([feat[i, 0], feat[i, 1]], axis=1)
        a_ref[span, :] = operand(x, True).T.astype(bf16)
        b_ref[:, span] = operand(x, False).astype(bf16)

    def form(t, row, cols):
        ds_ref[t % 2] = jnp.dot(a_ref[row * TILE : (row + 1) * TILE, :], cols, preferred_element_type=f32)
        for s in range(TILE // CHUNK):
            at = slice(s * CHUNK, (s + 1) * CHUNK)
            d2 = jnp.maximum(ds_ref[t % 2, at, :], 0.0) + 1e-6
            d = d2 * lax.rsqrt(d2)
            env = jnp.maximum(1.0 - d, 0.0)
            k = (1.0 + root_three * d) * jnp.exp2((-root_three * log2_e) * d) * (env * env)
            hi = k.astype(bf16)
            khi[t, at, :] = hi
            klo[t, at, :] = (k - hi.astype(f32)).astype(bf16)

    def to_rows(t, v):
        return jnp.dot(khi[t], v, preferred_element_type=f32) + jnp.dot(klo[t], v, preferred_element_type=f32)

    def upright(v):
        parts = two_parts(v).astype(f32)
        wide = jnp.concatenate([parts, jnp.zeros((LANES - 16, p_slots), f32)], axis=0)
        return wide.T.astype(bf16)

    def pick_rows(k):
        cand = OFF[k][1]
        lo = tall[cand * TILE : (cand + 1) * TILE, :]
        hi = tall[(cand + 1) * TILE : (cand + 2) * TILE, :]
        return jnp.where(start[k] == cand, lo, hi)

    def to_cols(t, v):
        return fold(
            jnp.dot(v, khi[t], preferred_element_type=f32)
            + jnp.dot(v, klo[t], preferred_element_type=f32)
        )

    for i in range(NT):
        form(i, i, b_ref[:, i * TILE : (i + 1) * TILE])
    hand_on(0)
    form(NT, 0, pick(b_ref, 0, True))
    hand_on(1)
    for i, pairs in ((0, (1, 2)), (1, (3, 4)), (2, (5,))):
        when_recv(has_up, c_hand[i])
        up_x = jnp.concatenate([up_feat[i, 0], up_feat[i, 1]], axis=1)
        b_ref[:, p_slots + i * TILE : p_slots + (i + 1) * TILE] = operand(up_x, False).astype(bf16)
        for k in pairs:
            form(NT + k, OFF[k][0], pick(b_ref, k, False))
        if i == 0:
            hand_on(2)

    def own(i):
        return vec[:, i * TILE : (i + 1) * TILE]

    def operate(v, out_ref, c_out, up_ref, c_up, in_ref):
        vec[:, :p_slots] = two_parts(v)
        tall[:p_slots, :] = upright(v)
        acc = [jnp.zeros((8, TILE), f32) for _ in range(2 * NT)]
        for k in range(1, 6):
            row, cand, _ = OFF[k]
            t = to_cols(NT + k, own(row))
            acc[cand] = acc[cand] + keep0[k] * t
            acc[cand + 1] = acc[cand + 1] + keep1[k] * t
        out_ref[...] = jnp.concatenate(acc[NT:], axis=1)
        when_start(has_up, c_out)
        for i in range(NT):
            acc[i] = acc[i] + to_cols(i, own(i))
        t = to_cols(NT, own(0))
        acc[1] = acc[1] + keep0[0] * t
        acc[2] = acc[2] + keep1[0] * t
        side = [(keep0[0] + keep1[0]) * to_rows(NT, pick_rows(0)), None, None]
        when_recv(has_up, c_up)
        tall[p_slots:, :] = upright(up_ref[...])
        for k in range(1, 6):
            row = OFF[k][0]
            t = (keep0[k] + keep1[k]) * to_rows(NT + k, pick_rows(k))
            side[row] = t if side[row] is None else side[row] + t
        for row in range(NT):
            acc[row] = acc[row] + fold(side[row].T[:16])
        when_recv(has_down, c_out)
        total = jnp.concatenate(acc[:NT], axis=1) + in_ref[...]
        return v + strength * live * total

    def start_sums(first, second, part, got, ssem, rsem):
        part[0:8, :] = jnp.broadcast_to(jnp.sum(first, axis=1, keepdims=True), (8, 128))
        part[8:16, :] = jnp.broadcast_to(jnp.sum(second, axis=1, keepdims=True), (8, 128))
        copies = []
        for k in range(1, n):
            c = pltpu.make_async_remote_copy(
                src_ref=part, dst_ref=got.at[k - 1], send_sem=ssem.at[k - 1], recv_sem=rsem.at[k - 1],
                device_id={"pairs": lax.rem(me + k, n)}, device_id_type=mesh_ids,
            )
            c.start()
            copies.append(c)
        return copies

    def end_sums(copies, part, got):
        total = part[...]
        for k, c in enumerate(copies):
            c.wait_recv()
            total = total + got[k]
        return total[0:8, 0:1], total[8:16, 0:1]

    w = operate(r0, out1, c_1, up_r, c_r, in1)
    w_buf[...] = w
    when_start(has_down, c_w)
    sums1 = start_sums(r0 * r0, r0 * w, part1, got1, psend1, precv1)
    u = operate(w, out2, c_2, up_w, c_w, in2)
    norm0, curve0 = end_sums(sums1, part1, got1)
    step0 = norm0 / curve0
    r1 = r0 - step0 * w
    applied = w - step0 * u
    sums2 = start_sums(r1 * r1, r1 * applied, part2, got2, psend2, precv2)
    norm1, curve1 = end_sums(sums2, part2, got2)
    rescale = norm1 / norm0
    step1 = norm1 / (curve1 - rescale * norm1 / step0)
    sol_ref[...] = step0 * r0 + step1 * (r1 + rescale * r0)
    res_ref[...] = r1 - step1 * (applied + rescale * w)

    @pl.when(has_down)
    def _():
        for c in (*c_feat, c_r, c_w):
            c.wait_send()

    @pl.when(has_up)
    def _():
        for c in (c_1, c_2, *c_hand):
            c.wait_send()

    for c in sums1 + sums2:
        c.wait_send()


def on_device(n, features, inv_scale, cluster_order, counts, tile_cols, targets):
    p_slots = features.shape[1]
    rhs_rows = targets.shape[0]
    strength = 0.95 / (2 * BAND * TILE)
    padded = targets
    if rhs_rows < 8:
        padded = jnp.concatenate([targets, jnp.ones((8 - rhs_rows, p_slots), f32)], axis=0)
    vmem = pl.BlockSpec(memory_space=pltpu.VMEM)
    hbm = pl.BlockSpec(memory_space=pltpu.HBM)
    smem = pl.BlockSpec(memory_space=pltpu.SMEM)
    field = pltpu.VMEM((8, p_slots), f32)
    dma = pltpu.SemaphoreType.DMA
    tiles = 9
    out = jax.ShapeDtypeStruct((8, p_slots), f32)
    sol, res = pl.pallas_call(
        functools.partial(body, n, strength),
        out_shape=(out, out),
        in_specs=[hbm, vmem, vmem, smem, smem, hbm],
        out_specs=(vmem, vmem),
        scratch_shapes=[
            pltpu.VMEM((FEAT, p_slots), f32),
            field,
            dma((2,)),
            pltpu.VMEM((NT, 2, FEAT, TILE // 2), f32),
            pltpu.VMEM((NT, 2, FEAT, TILE // 2), f32),
            field, field, field, field, field, field, field, field,
            pltpu.VMEM((16, 128), f32),
            pltpu.VMEM((n - 1, 16, 128), f32),
            pltpu.VMEM((16, 128), f32),
            pltpu.VMEM((n - 1, 16, 128), f32),
            pltpu.VMEM((p_slots, DEPTH), bf16),
            pltpu.VMEM((DEPTH, 2 * p_slots), bf16),
            pltpu.VMEM((2, TILE, TILE), f32),
            pltpu.VMEM((tiles, TILE, TILE), bf16),
            pltpu.VMEM((tiles, TILE, TILE), bf16),
            pltpu.VMEM((16, p_slots), bf16),
            pltpu.VMEM((2 * p_slots, LANES), bf16),
            dma((10,)), dma((10,)),
            dma((n - 1,)), dma((n - 1,)), dma((n - 1,)), dma((n - 1,)),
        ],
        compiler_params=pltpu.CompilerParams(
            collective_id=0, has_side_effects=True, vmem_limit_bytes=VMEM_ASK
        ),
    )(features, inv_scale[None, :], cluster_order.reshape(p_slots // LANES, LANES), counts, tile_cols.T, padded)
    return sol[:rhs_rows], res[:rhs_rows]


def solution(mesh):
    return jax.shard_map(
        functools.partial(on_device, mesh.shape["pairs"]),
        mesh=mesh,
        in_specs=(
            P(None, ("groups", "pairs")),
            P(),
            P(("groups", "pairs")),
            P(("groups", "pairs")),
            P("groups", None),
            P("rhs", ("groups", "pairs")),
        ),
        out_specs=(P("rhs", ("groups", "pairs")), P("rhs", ("groups", "pairs"))),
        check_vma=False,
    )
```
